256 devices in a mesh: wide: 32 (over x, y, core), narrow: 8 (over z).
Axes of the slice: x: 4, y: 4, z: 8, core: 2. Of those that a mesh axis runs over, the one named last changes fastest.
Arguments:
- hidden: bfloat16 [1024, 4, 8192], P('wide', None, 'narrow'), may hold values from -6 to 6
- shift_state: bfloat16 [1024, 3, 16384], P('narrow', None, 'wide'), may hold values from -6 to 6
- recurrent_row_state: bfloat16 [1024, 16, 16384], P('narrow', None, 'wide'), may hold values from -6 to 6
- input_codes: bfloat16 [8192, 2, 16384], P('narrow', None, 'wide'), may hold values from -4 to 4
- input_scales: float32 [64, 2, 128], P('narrow', None, 'wide'), may hold values from 0.0055242716 to 0.022097087
- filter_taps: float32 [4, 16384], P(None, 'wide'), may hold values from -0.5 to 0.5
- filter_bias: float32 [16384], P('wide'), may hold values from -0.5 to 0.5
- narrow_rank_weight: bfloat16 [16384, 512], P('wide'), may hold values from -0.046875 to 0.046875
- coefficient_weight: bfloat16 [16384, 32], P('wide'), may hold values from -0.046875 to 0.046875
- widen_weight: bfloat16 [512, 16384], P(None, 'wide'), may hold values from -0.25 to 0.25
- step_bias: float32 [16384], P('wide'), may hold values from -4 to -1
- decay_log: float32 [16, 16384], P(None, 'wide'), may hold values from 0 to 2.77
- skip_gain: float32 [16384], P('wide'), may hold values from 0.5 to 1.5
- output_codes: bfloat16 [16384, 8192], P('wide', 'narrow'), may hold values from -4 to 4
- output_scales: float32 [128, 64], P('wide', 'narrow'), may hold values from 0.00390625 to 0.015625
Outputs:
- mixed: bfloat16 [1024, 4, 8192], P('wide', None, 'narrow')
- shift_next: bfloat16 [1024, 3, 16384], P('narrow', None, 'wide')
- scan_next: bfloat16 [1024, 16, 16384], P('narrow', None, 'wide')
The draws below stay inside these ranges and needn't reach their ends.
All inputs are finite; a program needn't handle non-finite values.
Results may differ from the reference program's by a relative error of at most 0.04.
Values may be sent and summed in bfloat16 or wider, within the bound.
No kernel may reach another device: no remote copies, remote signals or barrier semaphores. Data moves between devices by JAX's collectives and lax.ppermute only.
A program may use at most 128 MiB of HBM per device.

```python
import math
import jax
import jax.numpy as jnp
from jax import lax

D = 8192
INNER = 16384
DSTATE = 16
DCONV = 4
DTRANK = 512
QB = 128
STEPS = 4
ROWS = 1024
N_WIDE = 32
N_NARROW = 8


def level_of(rng, dims, cuts, smallest, largest):
    def one(dim, shards_of):
        steps = jax.random.uniform(jax.random.fold_in(jax.random.fold_in(rng, 6), dim), (shards_of,), jnp.float32, smallest / len(cuts), largest / len(cuts))
        return jnp.repeat(jnp.exp(steps), dims[dim] // shards_of).reshape((-1,) + (1,) * (len(dims) - dim - 1))

    level = one(*cuts[0])
    for cut in cuts[1:]:
        level = level * one(*cut)
    return level


def gaussian(rng, extent, scale, bound, shards=(), kind=jnp.bfloat16):
    entries = jax.random.normal(rng, extent, jnp.float32) * scale
    if len(shards) > 0:
        entries = level_of(rng, extent, shards, -0.22, 0.18) * entries
    return jnp.clip(entries, min=-bound, max=bound).astype(kind)


def setup_inputs(seed: int = 0) -> dict:
    key_list = jax.random.split(jax.random.key(seed), 16)
    hidden = gaussian(key_list[0], (ROWS, STEPS, D), 1.0, 6.0, ((0, 32), (2, 8)))
    shift_state = gaussian(key_list[1], (ROWS, DCONV - 1, INNER), 1.0, 6.0, ((0, 8), (2, 32)))
    recurrent_row_state = gaussian(key_list[2], (ROWS, DSTATE, INNER), 1.0, 6.0, ((0, 8), (2, 32)))
    input_codes = gaussian(key_list[3], (D, 2, INNER), 1.0, 4.0, ((0, 8), (2, 32)))
    input_scales = jnp.clip(jnp.exp(math.log(0.022097087) - 1.3862944 * jax.random.uniform(key_list[4], (D // QB, 2, INNER // QB), jnp.float32) ** level_of(key_list[4], (D // QB, 2, INNER // QB), ((0, 8), (2, 32)), -0.2, 0.2)), 0.0055242716, 0.022097087)
    filter_taps = jnp.clip(jax.random.uniform(key_list[5], (DCONV, INNER), jnp.float32, -0.5, 0.5) * level_of(key_list[5], (DCONV, INNER), ((1, 32),), -0.4, 0.0), -0.5, 0.5)
    filter_bias = jnp.clip(jax.random.uniform(key_list[6], (INNER,), jnp.float32, -0.5, 0.5) * level_of(key_list[6], (INNER,), ((0, 32),), -0.4, 0.0), -0.5, 0.5)
    narrow_rank_weight = gaussian(key_list[7], (INNER, DTRANK), INNER ** -0.5, 0.046875, ((0, 32),))
    coefficient_weight = gaussian(key_list[8], (INNER, 2 * DSTATE), INNER ** -0.5, 0.046875, ((0, 32),))
    widen_weight = gaussian(key_list[9], (DTRANK, INNER), DTRANK ** -0.5, 0.25, ((1, 32),))
    step_bias = jnp.clip(-4.0 + 3.0 * jax.random.uniform(key_list[10], (INNER,), jnp.float32) ** level_of(key_list[10], (INNER,), ((0, 32),), -0.2, 0.2), -4.0, -1.0)
    decay_log = jnp.clip(2.77 * jax.random.uniform(key_list[11], (DSTATE, INNER), jnp.float32) ** level_of(key_list[11], (DSTATE, INNER), ((1, 32),), -0.2, 0.2), 0.0, 2.77)
    skip_gain = jnp.clip(0.5 + 1.0 * jax.random.uniform(key_list[12], (INNER,), jnp.float32) ** level_of(key_list[12], (INNER,), ((0, 32),), -0.2, 0.2), 0.5, 1.5)
    output_codes = gaussian(key_list[13], (INNER, D), 1.0, 4.0, ((0, 32), (1, 8)))
    output_scales = jnp.clip(jnp.exp(math.log(0.015625) - 1.3862944 * jax.random.uniform(key_list[14], (INNER // QB, D // QB), jnp.float32) ** level_of(key_list[14], (INNER // QB, D // QB), ((0, 32), (1, 8)), -0.2, 0.2)), 0.00390625, 0.015625)
    return {"hidden": hidden, "shift_state": shift_state, "recurrent_row_state": recurrent_row_state, "input_codes": input_codes, "input_scales": input_scales, "filter_taps": filter_taps, "filter_bias": filter_bias, "narrow_rank_weight": narrow_rank_weight, "coefficient_weight": coefficient_weight, "widen_weight": widen_weight, "step_bias": step_bias, "decay_log": decay_log, "skip_gain": skip_gain, "output_codes": output_codes, "output_scales": output_scales}


def dequantize(codes, scales):
    height, width = codes.shape
    blocks = codes.astype(jnp.float32).reshape(height // QB, QB, width // QB, QB) * scales[:, None, :, None]
    return blocks.reshape(height, width).astype(jnp.bfloat16)


def blocked_product(left, right, pieces):
    span = left.shape[1] // pieces

    def add_block(total, index):
        cols = lax.dynamic_slice_in_dim(left, (index * span).astype(jnp.int32), span, 1)
        rows_part = lax.dynamic_slice_in_dim(right, (index * span).astype(jnp.int32), span, 0)
        partial_value = jnp.dot(cols, rows_part, preferred_element_type=jnp.float32).astype(jnp.bfloat16)
        partial_value = lax.optimization_barrier(partial_value)
        return total + partial_value.astype(jnp.float32), None

    start = jnp.zeros((left.shape[0], right.shape[1]), jnp.float32)
    total, unused = lax.scan(add_block, start, jnp.arange(pieces, dtype=jnp.int32))
    return total.astype(jnp.bfloat16)


def reference(hidden, shift_state, recurrent_row_state, input_codes, input_scales, filter_taps, filter_bias, narrow_rank_weight, coefficient_weight, widen_weight, step_bias, decay_log, skip_gain, output_codes, output_scales):
    w_in = dequantize(input_codes.reshape(D, 2 * INNER), input_scales.reshape(D // QB, 2 * INNER // QB))
    w_out = dequantize(output_codes, output_scales)
    flat = hidden.reshape(ROWS * STEPS, D)
    xz = blocked_product(flat, w_in, N_NARROW).reshape(ROWS, STEPS, 2, INNER)
    lifted = xz[:, :, 0]
    gating = xz[:, :, 1]
    window_state = shift_state
    filtered_list = []
    for step in range(STEPS):
        window = jnp.concatenate([window_state, lifted[:, step][:, None]], axis=1)
        prior_value = jnp.sum(window.astype(jnp.float32) * filter_taps[None], axis=1) + filter_bias
        filtered_list.append(jax.nn.silu(prior_value).astype(jnp.bfloat16))
        window_state = window[:, 1:]
    convolved_input = jnp.stack(filtered_list, axis=1)
    filtered_flat = convolved_input.reshape(ROWS * STEPS, INNER)
    reduced = jnp.dot(filtered_flat, narrow_rank_weight, preferred_element_type=jnp.float32)
    coefficients = jnp.dot(filtered_flat, coefficient_weight, preferred_element_type=jnp.float32)
    lowered_precision16 = reduced.astype(jnp.bfloat16)
    delta = jax.nn.softplus(jnp.dot(lowered_precision16, widen_weight, preferred_element_type=jnp.float32) + step_bias)
    delta = delta.reshape(ROWS, STEPS, INNER)
    coefficients = coefficients.reshape(ROWS, STEPS, 2 * DSTATE)
    rates = -jnp.exp(decay_log)
    group = min(ROWS, 128)
    count = ROWS // group

    def scan_rows(items):
        state_rows, step_delta_rows, filt_rows, coef_rows, gate_rows = items
        recurrence = state_rows.astype(jnp.float32)
        outputs = []
        for step in range(STEPS):
            step_size = step_delta_rows[:, step]
            value = filt_rows[:, step].astype(jnp.float32)
            b_in = coef_rows[:, step, :DSTATE]
            c_out = coef_rows[:, step, DSTATE:]
            recurrence = jnp.exp(step_size[:, None, :] * rates[None]) * recurrence + (step_size * value)[:, None, :] * b_in[:, :, None]
            result = jnp.sum(c_out[:, :, None] * recurrence, axis=1) + skip_gain * value
            outputs.append((result * jax.nn.silu(gate_rows[:, step].astype(jnp.float32))).astype(jnp.bfloat16))
        return jnp.stack(outputs, axis=1), recurrence.astype(jnp.bfloat16)

    def grouped(array):
        return array.reshape((count, group) + array.shape[1:])

    output, scan_next = lax.map(scan_rows, (grouped(recurrent_row_state), grouped(delta), grouped(convolved_input), grouped(coefficients), grouped(gating)))
    output = output.reshape(ROWS * STEPS, INNER)
    scan_next = scan_next.reshape(ROWS, DSTATE, INNER)
    mixed = blocked_product(output, w_out, N_WIDE).reshape(ROWS, STEPS, D)
    return (mixed, window_state, scan_next)
```

```python
import jax
import jax.numpy as jnp
from jax import lax
from jax.experimental import pallas as pl
from jax.experimental.pallas import tpu as pltpu
from jax.sharding import PartitionSpec as P

QB = 128
NX, NY, NZ = 4, 4, 8
HALVES = 2
BF = jnp.bfloat16
F32 = jnp.float32


def dequantize(codes, scales):
    height, width = codes.shape
    blocks = (
        codes.astype(F32).reshape(height // QB, QB, width // QB, QB)
        * scales[:, None, :, None]
    )
    return blocks.reshape(height, width).astype(BF)


def wide_of(x, y, c):
    return ((x % NX) * NY + (y % NY)) * 2 + c


def swap_cores(a):
    return lax.ppermute(a, "wide", [(w, w ^ 1) for w in range(2 * NX * NY)])


def ring(a):
    pairs = [
        (w * NZ + z, w * NZ + (z + (1 if w % 2 == 0 else -1)) % NZ)
        for w in range(2 * NX * NY)
        for z in range(NZ)
    ]
    return lax.ppermute(a, ("wide", "narrow"), pairs)


def shift(a, step, first):
    pairs = []
    for x in range(NX):
        for y in range(NY):
            for c in range(2):
                if (c == 0) == first:
                    pairs.append((wide_of(x, y, c), wide_of(x + step, y, c)))
                else:
                    pairs.append((wide_of(x, y, c), wide_of(x, y + step, c)))
    return lax.ppermute(a, "wide", pairs)


def pick_blocks(source, index):
    count = index.shape[0]

    def kernel(index_ref, source_ref, out_ref):
        for i in range(count):
            out_ref[i] = source_ref[index_ref[i]]

    nbytes = 2 * count * source.size // source.shape[0] * source.dtype.itemsize
    return pl.pallas_call(
        kernel,
        out_shape=jax.ShapeDtypeStruct((count,) + source.shape[1:], source.dtype),
        in_specs=[
            pl.BlockSpec(memory_space=pltpu.SMEM),
            pl.BlockSpec(memory_space=pltpu.VMEM),
        ],
        out_specs=pl.BlockSpec(memory_space=pltpu.VMEM),
        compiler_params=pltpu.CompilerParams(vmem_limit_bytes=16 * 1024 * 1024),
        cost_estimate=pl.CostEstimate(flops=0, bytes_accessed=nbytes, transcendentals=0),
    )(index.astype(jnp.int32), source)


def dot(a, b):
    return jnp.dot(a, b, preferred_element_type=F32)


def local(
    hidden,
    shift_state,
    recurrent_row_state,
    input_codes,
    input_scales,
    filter_taps,
    filter_bias,
    narrow_rank_weight,
    coefficient_weight,
    widen_weight,
    step_bias,
    decay_log,
    skip_gain,
    output_codes,
    output_scales,
):
    rows, steps, depth = hidden.shape
    channels = input_codes.shape[2]
    part = rows // HALVES
    tok = part * steps
    taps = filter_taps.shape[0]
    states = decay_log.shape[0]
    rank = narrow_rank_weight.shape[1]
    model = output_codes.shape[1]

    wide = lax.axis_index("wide")
    z = lax.axis_index("narrow")
    core = wide % 2
    x, y = wide // (2 * NY), (wide // 2) % NY
    first_core = core == 0
    sign = 1 - 2 * core
    u = jnp.where(first_core, x, y)
    v = jnp.where(first_core, y, x)

    def by_core(a, b):
        return jnp.where(first_core, a, b), jnp.where(first_core, b, a)

    w_in = dequantize(input_codes.reshape(depth, 2 * channels), input_scales.reshape(input_scales.shape[0], -1))
    w_out = dequantize(output_codes, output_scales)
    w_in_other = swap_cores(w_in)
    w_out_other = swap_cores(w_out)
    weight = [
        jnp.concatenate([w_in[:, p * channels : (p + 1) * channels], w_in_other[:, p * channels : (p + 1) * channels]], axis=1)
        for p in range(2)
    ]
    weight_own = [w_in[:, p * channels : (p + 1) * channels] for p in range(2)]
    w_down = jnp.concatenate(by_core(w_out, w_out_other), axis=0)

    tokens = hidden.reshape(HALVES, part, steps, depth).transpose(0, 2, 1, 3).reshape(HALVES, tok, depth)
    plane = (z + sign * jnp.arange(-3, 5)) % NZ
    want_x = jnp.repeat(plane // 2, 2)
    want_y = (2 * (plane % 2)[:, None] + jnp.arange(2)[None]).reshape(-1)
    want_u = jnp.where(first_core, want_x, want_y)
    want_v = jnp.where(first_core, want_y, want_x)
    gather_index = ((want_v - v) % 4) * 4 + (want_u - u) % 4

    def gather_rows(block):
        one = jnp.stack([block, shift(block, -1, True), shift(block, 2, True), shift(block, 1, True)])
        two = jnp.concatenate([one, shift(one, -1, False), shift(one, 2, False), shift(one, 1, False)])
        mine = pick_blocks(two, gather_index).reshape(8, 2 * tok, depth)
        other = swap_cores(mine[:4])
        left = [jnp.concatenate([mine[3 + k], other[3 - k]]) for k in range(4)]
        left.append(mine[7])
        return left

    def sum_over_z(left, p):
        acc = dot(left[4], weight[p]).astype(BF)
        got = ring(acc)
        acc = dot(left[3], weight[p])
        acc = jnp.concatenate([acc[: 2 * tok] + got.astype(F32), acc[2 * tok :]]).astype(BF)
        got = ring(acc)
        for k in (2, 1):
            acc = (dot(left[k], weight[p]) + got.astype(F32)).astype(BF)
            got = ring(acc)
        other = swap_cores(got[:, channels:])
        total = dot(left[0], weight_own[p]) + got[:, :channels].astype(F32)
        total = total + jnp.concatenate([other[2 * tok :], other[: 2 * tok]]).astype(F32)
        total = total.astype(BF)
        return jnp.stack(by_core(total[: 2 * tok], total[2 * tok :])).reshape(2, 2, steps, part, channels)

    def halves_of(a):
        b = a.reshape((2, 2, HALVES, part) + a.shape[1:])
        return [jnp.swapaxes(b[:, :, h], 0, 1) for h in range(HALVES)]

    def rows_of(parts):
        b = jnp.stack([jnp.swapaxes(q, 0, 1) for q in parts], axis=2)
        return b.reshape((4 * rows,) + b.shape[4:])

    lefts = [gather_rows(tokens[h]) for h in range(HALVES)]
    lifted = [sum_over_z(lefts[h], 0) for h in range(HALVES)]
    gating = [sum_over_z(lefts[h], 1) for h in range(HALVES)]

    shift_parts = halves_of(shift_state)
    filtered, window_next = [], []
    for h in range(HALVES):
        window = [shift_parts[h][:, :, :, k] for k in range(taps - 1)] + [lifted[h][:, :, t] for t in range(steps)]
        outs = []
        for t in range(steps):
            prior = filter_bias
            for k in range(taps):
                prior = prior + window[t + k].astype(F32) * filter_taps[k]
            outs.append(jax.nn.silu(prior).astype(BF))
        filtered.append(jnp.stack(outs, axis=2))
        window_next.append(jnp.stack(window[steps:], axis=3))
    shift_next = rows_of(window_next)

    narrow = jnp.concatenate([narrow_rank_weight, coefficient_weight], axis=1)
    width = narrow.shape[1]
    small = jnp.stack([dot(f.reshape(-1, channels), narrow).astype(BF) for f in filtered])
    small = small.reshape(HALVES, 2, 2 * tok, width)
    keep, give = by_core(small[:, 0], small[:, 1])
    total = (keep.astype(F32) + swap_cores(give).astype(F32)).astype(BF)
    for first in (True, False):
        others = [shift(total, d, first) for d in (1, -1, 2)]
        total = sum([o.astype(F32) for o in others], total.astype(F32)).astype(BF)
    total_other = swap_cores(total)
    small = jnp.stack(by_core(total, total_other), axis=1)
    reduced = small[..., :rank].reshape(HALVES, 4 * tok, rank)
    coefficients = small[..., rank:].astype(F32).reshape(HALVES, 2, 2, steps, part, 2 * states)

    rates = -jnp.exp(decay_log)
    state_parts = halves_of(recurrent_row_state)
    scan_parts, mixed_parts = [], []
    for h in range(HALVES):
        delta = jax.nn.softplus(dot(reduced[h], widen_weight) + step_bias)
        delta = delta.reshape(2, 2, steps, part, channels)
        state = state_parts[h].astype(F32)
        outs = []
        for t in range(steps):
            step_size = delta[:, :, t]
            value = filtered[h][:, :, t].astype(F32)
            b_in = coefficients[h][:, :, t, :, :states]
            c_out = coefficients[h][:, :, t, :, states:]
            state = (
                jnp.exp(step_size[:, :, :, None, :] * rates) * state
                + (step_size * value)[:, :, :, None, :] * b_in[..., None]
            )
            result = jnp.sum(c_out[..., None] * state, axis=3) + skip_gain * value
            outs.append((result * jax.nn.silu(gating[h][:, :, t].astype(F32))).astype(BF))
        scan_parts.append(state.astype(BF))
        output = jnp.stack(outs, axis=2).reshape(4 * tok, channels)

        output = jnp.concatenate(by_core(output, swap_cores(output)), axis=1)
        mine, theirs = by_core(output[: 2 * tok], output[2 * tok :])
        block = jnp.concatenate([mine, theirs])
        known = [mine]
        for k in range(3):
            block = ring(block)
            known.append(block[: 2 * tok])
            theirs = block[2 * tok :]
            known.insert(0, swap_cores(theirs))
        known.append(ring(block[: 2 * tok]))
        known = jnp.concatenate(known).reshape(16, tok, 2 * channels)
        e, f = jnp.arange(16) // 4, jnp.arange(16) % 4
        to_u, to_v = (u + e) % 4, (v + f) % 4
        to_x = jnp.where(first_core, to_u, to_v)
        to_y = jnp.where(first_core, to_v, to_u)
        to_plane = 2 * to_x + to_y // 2
        slot = (sign * (z - to_plane) + 3) % NZ
        picked = pick_blocks(known, slot * 2 + to_y % 2).reshape(16 * tok, 2 * channels)
        part_sums = dot(picked, w_down).astype(BF).reshape(4, 4 * tok, model)
        total = part_sums[0].astype(F32)
        for e, d in ((1, 1), (2, 2), (3, -1)):
            total = total + shift(part_sums[e], d, True).astype(F32)
        total = total.astype(BF).reshape(4, tok, model)
        final = total[0].astype(F32)
        for e, d in ((1, 1), (2, 2), (3, -1)):
            final = final + shift(total[e], d, False).astype(F32)
        mixed_parts.append(final.astype(BF).reshape(steps, part, model))

    mixed = jnp.stack(mixed_parts).transpose(0, 2, 1, 3).reshape(rows, steps, model)
    return (mixed, shift_next, rows_of(scan_parts))


def solution(mesh):
    return jax.shard_map(
        local,
        mesh=mesh,
        in_specs=(
            P("wide", None, "narrow"),
            P("narrow", None, "wide"),
            P("narrow", None, "wide"),
            P("narrow", None, "wide"),
            P("narrow", None, "wide"),
            P(None, "wide"),
            P("wide"),
            P("wide", None),
            P("wide", None),
            P(None, "wide"),
            P("wide"),
            P(None, "wide"),
            P("wide"),
            P("wide", "narrow"),
            P("wide", "narrow"),
        ),
        out_specs=(P("wide", None, "narrow"), P("narrow", None, "wide"), P("narrow", None, "wide")),
        check_vma=False,
    )
```

```python
import math

import jax
import jax.numpy as jnp
from jax import lax
from jax.experimental import pallas as pl
from jax.experimental.pallas import tpu as pltpu
from jax.sharding import PartitionSpec as P

QB = 128
NX, NY, NZ = 4, 4, 8
HALVES = 2
SPANS = 1
BF = jnp.bfloat16
F32 = jnp.float32


def dequantize(codes, scales):
    height, width = codes.shape
    blocks = (
        codes.astype(F32).reshape(height // QB, QB, width // QB, QB)
        * scales[:, None, :, None]
    )
    return blocks.reshape(height, width).astype(BF)


def wide_of(x, y, c):
    return ((x % NX) * NY + (y % NY)) * 2 + c


def swap_cores(a):
    return lax.ppermute(a, "wide", [(w, w ^ 1) for w in range(2 * NX * NY)])


def ring(a):
    pairs = [
        (w * NZ + z, w * NZ + (z + (1 if w % 2 == 0 else -1)) % NZ)
        for w in range(2 * NX * NY)
        for z in range(NZ)
    ]
    return lax.ppermute(a, ("wide", "narrow"), pairs)


def shift(a, step, first):
    pairs = []
    for x in range(NX):
        for y in range(NY):
            for c in range(2):
                if (c == 0) == first:
                    pairs.append((wide_of(x, y, c), wide_of(x + step, y, c)))
                else:
                    pairs.append((wide_of(x, y, c), wide_of(x, y + step, c)))
    return lax.ppermute(a, "wide", pairs)


def pick_blocks(sources, index):
    count = index.shape[0]
    pieces = len(sources)

    def kernel(index_ref, *refs):
        for i in range(count):
            for j in range(pieces):
                refs[-1][i, j] = refs[j][index_ref[i]]

    shape = (count, pieces) + sources[0].shape[1:]
    return pl.pallas_call(
        kernel,
        out_shape=jax.ShapeDtypeStruct(shape, sources[0].dtype),
        in_specs=[pl.BlockSpec(memory_space=pltpu.SMEM)] + [pl.BlockSpec(memory_space=pltpu.VMEM)] * pieces,
        out_specs=pl.BlockSpec(memory_space=pltpu.VMEM),
        compiler_params=pltpu.CompilerParams(vmem_limit_bytes=16 * 1024 * 1024),
        cost_estimate=pl.CostEstimate(flops=0, bytes_accessed=4 * math.prod(shape), transcendentals=0),
    )(index.astype(jnp.int32), *sources)


def causal_filter(pieces, window, taps, bias, narrow):
    blocks, span, part, channels = pieces[0].shape
    steps = span * len(pieces)
    width = narrow.shape[1]
    count = taps.shape[0]

    def kernel(*refs):
        piece_refs = refs[: len(pieces)]
        window_ref, taps_ref, bias_ref, narrow_ref, filtered_ref, small_ref = refs[len(pieces) :]
        for b in range(blocks):
            inputs = [window_ref[k, b].astype(F32) for k in range(count - 1)]
            inputs += [ref[b, t].astype(F32) for ref in piece_refs for t in range(span)]
            for t in range(steps):
                prior = bias_ref[...] + inputs[t] * taps_ref[0:1]
                for k in range(1, count):
                    prior = prior + inputs[t + k] * taps_ref[k : k + 1]
                filtered_ref[b, t] = (prior * jax.nn.sigmoid(prior)).astype(BF)
        left = filtered_ref[...].reshape(blocks * steps * part, channels)
        small_ref[...] = jnp.dot(left, narrow_ref[...], preferred_element_type=F32).astype(BF)

    return pl.pallas_call(
        kernel,
        out_shape=(
            jax.ShapeDtypeStruct((blocks, steps, part, channels), BF),
            jax.ShapeDtypeStruct((blocks * steps * part, width), BF),
        ),
        compiler_params=pltpu.CompilerParams(vmem_limit_bytes=16 * 1024 * 1024),
        cost_estimate=pl.CostEstimate(
            flops=2 * blocks * steps * part * channels * width,
            bytes_accessed=2 * 1024 * 1024,
            transcendentals=blocks * steps * part * channels,
        ),
    )(*pieces, window, taps, bias.reshape(1, -1), narrow)


def selective_scan(small, filtered, state, widen, bias, decay_log, skip):
    blocks, steps, part, channels = filtered.shape
    states = decay_log.shape[0]
    rank = widen.shape[0]
    tile = 256
    tiles = channels // tile

    def kernel(small_ref, filtered_ref, state_ref, widen_ref, bias_ref, decay_ref, skip_ref, result_ref, next_ref, delta_ref, rates_ref):
        value = jnp.dot(small_ref[:, :rank], widen_ref[...], preferred_element_type=F32) + bias_ref[...]
        delta_ref[...] = (jnp.maximum(value, 0.0) + jnp.log1p(jnp.exp(-jnp.abs(value)))).reshape(blocks, steps, part, channels)
        rates_ref[...] = jnp.exp(decay_ref[...]) * (-1.4426950408889634)

        def body(i, carry):
            b = i // tiles
            cols = pl.ds(pl.multiple_of((i % tiles) * tile, tile), tile)
            deltas, inputs, sums = [], [], []
            for t in range(steps):
                x = filtered_ref[b, t, :, cols].astype(F32)
                d = delta_ref[b, t, :, cols]
                deltas.append(d)
                inputs.append(d * x)
                sums.append(skip_ref[:, cols] * x)
            coefs = [
                small_ref[pl.ds(pl.multiple_of((b * steps + t) * part, part), part), rank : rank + 2 * states].astype(F32)
                for t in range(steps)
            ]
            for n in range(states):
                s = state_ref[n, b, :, cols].astype(F32)
                rate = rates_ref[n : n + 1, cols]
                for t in range(steps):
                    s = jnp.exp2(deltas[t] * rate) * s + inputs[t] * coefs[t][:, n : n + 1]
                    sums[t] = sums[t] + s * coefs[t][:, states + n : states + n + 1]
                next_ref[n, b, :, cols] = s.astype(BF)
            for t in range(steps):
                result_ref[b, t, :, cols] = sums[t]
            return carry

        lax.fori_loop(0, blocks * tiles, body, 0)

    tokens = blocks * steps * part
    return pl.pallas_call(
        kernel,
        out_shape=(
            jax.ShapeDtypeStruct(filtered.shape, F32),
            jax.ShapeDtypeStruct(state.shape, BF),
        ),
        scratch_shapes=[
            pltpu.VMEM(filtered.shape, F32),
            pltpu.VMEM((states, channels), F32),
        ],
        compiler_params=pltpu.CompilerParams(vmem_limit_bytes=24 * 1024 * 1024),
        cost_estimate=pl.CostEstimate(
            flops=2 * tokens * channels * (rank + 4 * states), bytes_accessed=12 * 1024 * 1024, transcendentals=tokens * channels * states
        ),
    )(small, filtered, state, widen, bias.reshape(1, -1), decay_log, skip.reshape(1, -1))


def after(a, b):
    return lax.optimization_barrier((a, b))[0]


def dot(a, b):
    return jnp.dot(a, b, preferred_element_type=F32)


def local(
    hidden,
    shift_state,
    recurrent_row_state,
    input_codes,
    input_scales,
    filter_taps,
    filter_bias,
    narrow_rank_weight,
    coefficient_weight,
    widen_weight,
    step_bias,
    decay_log,
    skip_gain,
    output_codes,
    output_scales,
):
    rows, steps, depth = hidden.shape
    part = rows // HALVES
    span = steps // SPANS
    tok = part * span
    chunks = HALVES * SPANS
    channels = input_codes.shape[2]
    taps = filter_taps.shape[0]
    model = output_codes.shape[1]

    wide = lax.axis_index("wide")
    z = lax.axis_index("narrow")
    core = wide % 2
    x, y = wide // (2 * NY), (wide // 2) % NY
    first_core = core == 0
    sign = 1 - 2 * core
    u = jnp.where(first_core, x, y)
    v = jnp.where(first_core, y, x)

    def by_core(a, b):
        return jnp.where(first_core, a, b), jnp.where(first_core, b, a)

    tokens = hidden.reshape(HALVES, part, steps, depth).transpose(0, 2, 1, 3).reshape(chunks, tok, depth)
    plane = (z + sign * jnp.arange(-3, 5)) % NZ
    want_x = jnp.repeat(plane // 2, 2)
    want_y = (2 * (plane % 2)[:, None] + jnp.arange(2)[None]).reshape(-1)
    want_u = jnp.where(first_core, want_x, want_y)
    want_v = jnp.where(first_core, want_y, want_x)
    gather_index = ((want_v - v) % 4) * 4 + (want_u - u) % 4

    def gather_rows(block, start=None):
        one = jnp.stack([block, shift(block, -1, True), shift(block, 2, True), shift(block, 1, True)])
        up, down = shift(one, -1, False), shift(one, 1, False)
        far = jnp.concatenate([shift(up[:2], -1, False), shift(down[2:], 1, False)])
        two = jnp.concatenate([one, up, far, down])
        if start is not None:
            two = after(two, start)
        mine = pick_blocks([two], gather_index)[:, 0]
        other = swap_cores(mine[:8])
        return mine, other, one, up

    def unpack(mine, other, i):
        return mine[:, i].reshape(8, 2 * tok, depth), other[:, i].reshape(4, 2 * tok, depth)

    token = [None]

    def seq(a):
        if token[0] is not None:
            a = after(a, token[0])
        token[0] = a
        return a

    def sum_over_z(mine, other, p, start=None):
        if start is not None:
            mine = after(mine, start)
        size = mine.shape[1]
        ahead = dot(mine[3:].reshape(5 * size, depth), weight[p]).astype(BF).reshape(5, size, 2 * channels)
        also = dot(other.reshape(4 * size, depth), weight[p]).astype(BF).reshape(4, size, 2 * channels)
        got = ring(ahead[4])
        gots = [got]
        acc = jnp.concatenate([(ahead[3].astype(F32) + got.astype(F32)).astype(BF), also[0]])
        for k in (2, 1):
            got = ring(acc)
            gots.append(got)
            acc = (jnp.concatenate([ahead[k], also[3 - k]]).astype(F32) + got.astype(F32)).astype(BF)
        got = ring(acc)
        swapped = swap_cores(got[:, channels:])
        total = jnp.concatenate([ahead[0], also[3]])[:, :channels].astype(F32) + got[:, :channels].astype(F32)
        total = total + jnp.concatenate([swapped[size:], swapped[:size]]).astype(F32)
        total = total.astype(BF)
        return jnp.concatenate(by_core(total[:size], total[size:])).reshape(4, span, part, channels), gots

    def halves_of(a):
        k = a.shape[1]
        b = a.reshape((2, 2, HALVES, part, k, channels)).transpose(2, 4, 1, 0, 3, 5)
        return [b[h].reshape(k, 4, part, channels) for h in range(HALVES)]

    def rows_of(parts):
        k = parts[0].shape[0]
        b = jnp.stack(parts).reshape(HALVES, k, 2, 2, part, channels)
        return b.transpose(3, 2, 0, 4, 1, 5).reshape(4 * rows, k, channels)

    mine, other, one, up = gather_rows(tokens[:SPANS])

    input_codes = after(input_codes, one)
    w_in = dequantize(input_codes.reshape(depth, 2 * channels), input_scales.reshape(input_scales.shape[0], -1))
    w_in_other = swap_cores(w_in)
    weight = [
        jnp.concatenate([w_in[:, p * channels : (p + 1) * channels], w_in_other[:, p * channels : (p + 1) * channels]], axis=1)
        for p in range(2)
    ]

    lifted, gating, gots, lefts = [], [], [], []
    for h in range(HALVES):
        if h > 0:
            mine, other, one, up = gather_rows(after(tokens[h : h + 1], one))
        lefts.append(unpack(mine, other, 0))
        total, got = sum_over_z(*lefts[h], 0)
        lifted.append(total)
        gots.append(got)
    for h in range(HALVES):
        gating.append(sum_over_z(*lefts[h], 1, gots[h][2])[0])

    shift_state, recurrent_row_state = after((shift_state, recurrent_row_state), gots[0][0])
    w_out = dequantize(after(output_codes, gots[0][1]), output_scales)
    w_down = jnp.concatenate(by_core(w_out, swap_cores(w_out)), axis=0)

    narrow = jnp.concatenate([narrow_rank_weight, coefficient_weight], axis=1)
    width = narrow.shape[1]
    windows = halves_of(shift_state)
    filtered, smalls = [], []
    for h in range(HALVES):
        f, small = causal_filter(lifted[h : h + 1], windows[h], filter_taps, filter_bias, narrow)
        filtered.append(f)
        smalls.append(small)
    small = jnp.stack(smalls)
    mid = small.shape[1] // 2
    keep, give = by_core(small[:, :mid], small[:, mid:])
    total = (keep.astype(F32) + swap_cores(give).astype(F32)).astype(BF)
    for first in (True, False):
        others = [shift(total, d, first) for d in (1, -1, 2)]
        total = sum([o.astype(F32) for o in others], total.astype(F32)).astype(BF)
    smalls = jnp.concatenate(by_core(total, swap_cores(total)), axis=1)
    whole = [jnp.concatenate(lifted[h * SPANS : (h + 1) * SPANS], axis=1) for h in range(HALVES)]
    shift_next = rows_of([jnp.swapaxes(q[:, steps - taps + 1 :], 0, 1) for q in whole])

    state_parts = halves_of(recurrent_row_state)
    scan_parts = []
    e, f = jnp.arange(16) // 4, jnp.arange(16) % 4
    to_u, to_v = (u + e) % 4, (v + f) % 4
    to_x = jnp.where(first_core, to_u, to_v)
    to_y = jnp.where(first_core, to_v, to_u)
    slot = (sign * (z - 2 * to_x - to_y // 2) + 3) % NZ
    target = slot * 2 + to_y % 2

    results = []
    for h in range(HALVES):
        result, state = selective_scan(
            smalls[h], filtered[h], state_parts[h], widen_weight, step_bias, decay_log, skip_gain
        )
        scan_parts.append(state)
        results.append(result)

    pairs = 2
    duo = tok // pairs
    blocks, known, others = [], [], []
    for h in range(HALVES):
        output = (results[h] * jax.nn.silu(gating[h].astype(F32))).astype(BF).reshape(4 * tok, channels)
        output = jnp.concatenate(by_core(output, swap_cores(output)), axis=1)
        mine, theirs = by_core(output[: 2 * tok], output[2 * tok :])
        both = jnp.stack([mine, theirs]).reshape(4, pairs, duo, 2 * channels)
        blocks.append([both[:, i].reshape(4 * duo, 2 * channels) for i in range(pairs)])
        known.append([[b[: 2 * duo]] for b in blocks[h]])
        others.append([[], []])

    def send(h):
        blocks[h] = [ring(seq(b)) for b in blocks[h]]

    def forward(h, k):
        for i in range(pairs):
            block = seq(blocks[h][i])
            known[h][i].append(block[: 2 * duo])
            others[h][i].insert(0, block[2 * duo :])
            blocks[h][i] = ring(block if k < 2 else block[: 2 * duo])

    def exchange(h):
        count = 3 * 2 * duo
        got = swap_cores(jnp.concatenate(others[h][0] + others[h][1]))
        others[h] = [got[:count], got[count:]]

    def project(h):
        pieces = [
            jnp.concatenate([others[h][i]] + known[h][i] + [seq(blocks[h][i])]).reshape(16, duo, 2 * channels)
            for i in range(pairs)
        ]
        picked = pick_blocks(pieces, target).reshape(16 * tok, 2 * channels)
        return seq(dot(picked, w_down).astype(BF)).reshape(4, 4 * tok, model)

    send(0)
    send(1)
    for k in range(3):
        for h in range(HALVES):
            forward(h, k)
    for h in range(HALVES):
        exchange(h)

    low = project(0)
    from_low = shift(low[2], 1, True)
    high = project(1)
    from_high = shift(high[2], -1, True)
    up = jnp.concatenate([(low[1].astype(F32) + from_low.astype(F32)).astype(BF), high[1]])
    down = jnp.concatenate([low[3], (high[3].astype(F32) + from_high.astype(F32)).astype(BF)])
    total = jnp.concatenate([low[0], high[0]]).astype(F32)
    total = total + shift(up, 1, True).astype(F32) + shift(down, -1, True).astype(F32)
    total = total.astype(BF).reshape(2, 4, tok, model)
    final = total[:, 0].astype(F32)
    for f, d in ((1, 1), (2, 2), (3, -1)):
        final = final + shift(total[:, f], d, False).astype(F32)

    mixed = final.astype(BF).reshape(HALVES, steps, part, model).transpose(0, 2, 1, 3).reshape(rows, steps, model)
    return (mixed, shift_next, rows_of(scan_parts))


def solution(mesh):
    return jax.shard_map(
        local,
        mesh=mesh,
        in_specs=(
            P("wide", None, "narrow"),
            P("narrow", None, "wide"),
            P("narrow", None, "wide"),
            P("narrow", None, "wide"),
            P("narrow", None, "wide"),
            P(None, "wide"),
            P("wide"),
            P("wide", None),
            P("wide", None),
            P(None, "wide"),
            P("wide"),
            P(None, "wide"),
            P("wide"),
            P("wide", "narrow"),
            P("wide", "narrow"),
        ),
        out_specs=(P("wide", None, "narrow"), P("narrow", None, "wide"), P("narrow", None, "wide")),
        check_vma=False,
    )
```

```python
import math

import jax
import jax.numpy as jnp
from jax import lax
from jax.experimental import pallas as pl
from jax.experimental.pallas import tpu as pltpu
from jax.sharding import PartitionSpec as P

QB = 128
NX, NY, NZ = 4, 4, 8
HALVES = 2
SPANS = 1
BF = jnp.bfloat16
F32 = jnp.float32


def dequantize(codes, scales):
    height, width = codes.shape
    blocks = (
        codes.astype(F32).reshape(height // QB, QB, width // QB, QB)
        * scales[:, None, :, None]
    )
    return blocks.reshape(height, width).astype(BF)


def wide_of(x, y, c):
    return ((x % NX) * NY + (y % NY)) * 2 + c


def swap_cores(a):
    return lax.ppermute(a, "wide", [(w, w ^ 1) for w in range(2 * NX * NY)])


def ring(a):
    pairs = [
        (w * NZ + z, w * NZ + (z + (1 if w % 2 == 0 else -1)) % NZ)
        for w in range(2 * NX * NY)
        for z in range(NZ)
    ]
    return lax.ppermute(a, ("wide", "narrow"), pairs)


def shift(a, step, first):
    pairs = []
    for x in range(NX):
        for y in range(NY):
            for c in range(2):
                if (c == 0) == first:
                    pairs.append((wide_of(x, y, c), wide_of(x + step, y, c)))
                else:
                    pairs.append((wide_of(x, y, c), wide_of(x, y + step, c)))
    return lax.ppermute(a, "wide", pairs)


def pick_blocks(sources, index):
    count = index.shape[0]
    pieces = len(sources)

    def kernel(index_ref, *refs):
        for i in range(count):
            for j in range(pieces):
                refs[-1][i, j] = refs[j][index_ref[i]]

    shape = (count, pieces) + sources[0].shape[1:]
    return pl.pallas_call(
        kernel,
        out_shape=jax.ShapeDtypeStruct(shape, sources[0].dtype),
        in_specs=[pl.BlockSpec(memory_space=pltpu.SMEM)] + [pl.BlockSpec(memory_space=pltpu.VMEM)] * pieces,
        out_specs=pl.BlockSpec(memory_space=pltpu.VMEM),
        compiler_params=pltpu.CompilerParams(vmem_limit_bytes=16 * 1024 * 1024),
        cost_estimate=pl.CostEstimate(flops=0, bytes_accessed=4 * math.prod(shape), transcendentals=0),
    )(index.astype(jnp.int32), *sources)


def causal_filter(pieces, window, taps, bias, narrow):
    blocks, span, part, channels = pieces[0].shape
    steps = span * len(pieces)
    width = narrow.shape[1]
    count = taps.shape[0]

    def kernel(*refs):
        piece_refs = refs[: len(pieces)]
        window_ref, taps_ref, bias_ref, narrow_ref, filtered_ref, small_ref = refs[len(pieces) :]
        for b in range(blocks):
            inputs = [window_ref[k, b].astype(F32) for k in range(count - 1)]
            inputs += [ref[b, t].astype(F32) for ref in piece_refs for t in range(span)]
            for t in range(steps):
                prior = bias_ref[...] + inputs[t] * taps_ref[0:1]
                for k in range(1, count):
                    prior = prior + inputs[t + k] * taps_ref[k : k + 1]
                filtered_ref[b, t] = (prior * jax.nn.sigmoid(prior)).astype(BF)
        left = filtered_ref[...].reshape(blocks * steps * part, channels)
        small_ref[...] = jnp.dot(left, narrow_ref[...], preferred_element_type=F32).astype(BF)

    return pl.pallas_call(
        kernel,
        out_shape=(
            jax.ShapeDtypeStruct((blocks, steps, part, channels), BF),
            jax.ShapeDtypeStruct((blocks * steps * part, width), BF),
        ),
        compiler_params=pltpu.CompilerParams(vmem_limit_bytes=16 * 1024 * 1024),
        cost_estimate=pl.CostEstimate(
            flops=2 * blocks * steps * part * channels * width,
            bytes_accessed=2 * 1024 * 1024,
            transcendentals=blocks * steps * part * channels,
        ),
    )(*pieces, window, taps, bias.reshape(1, -1), narrow)


def selective_scan(small, filtered, state, widen, bias, decay_log, skip):
    blocks, steps, part, channels = filtered.shape
    states = decay_log.shape[0]
    rank = widen.shape[0]
    tile = 256
    tiles = channels // tile

    def kernel(small_ref, filtered_ref, state_ref, widen_ref, bias_ref, decay_ref, skip_ref, result_ref, next_ref, delta_ref, rates_ref):
        value = jnp.dot(small_ref[:, :rank], widen_ref[...], preferred_element_type=F32) + bias_ref[...]
        delta_ref[...] = (jnp.maximum(value, 0.0) + jnp.log1p(jnp.exp(-jnp.abs(value)))).reshape(blocks, steps, part, channels)
        rates_ref[...] = jnp.exp(decay_ref[...]) * (-1.4426950408889634)

        def body(i, carry):
            b = i // tiles
            cols = pl.ds(pl.multiple_of((i % tiles) * tile, tile), tile)
            deltas, inputs, sums = [], [], []
            for t in range(steps):
                x = filtered_ref[b, t, :, cols].astype(F32)
                d = delta_ref[b, t, :, cols]
                deltas.append(d)
                inputs.append(d * x)
                sums.append(skip_ref[:, cols] * x)
            coefs = [
                small_ref[pl.ds(pl.multiple_of((b * steps + t) * part, part), part), rank : rank + 2 * states].astype(F32)
                for t in range(steps)
            ]
            for n in range(states):
                s = state_ref[n, b, :, cols].astype(F32)
                rate = rates_ref[n : n + 1, cols]
                for t in range(steps):
                    s = jnp.exp2(deltas[t] * rate) * s + inputs[t] * coefs[t][:, n : n + 1]
                    sums[t] = sums[t] + s * coefs[t][:, states + n : states + n + 1]
                next_ref[n, b, :, cols] = s.astype(BF)
            for t in range(steps):
                result_ref[b, t, :, cols] = sums[t]
            return carry

        lax.fori_loop(0, blocks * tiles, body, 0)

    tokens = blocks * steps * part
    return pl.pallas_call(
        kernel,
        out_shape=(
            jax.ShapeDtypeStruct(filtered.shape, F32),
            jax.ShapeDtypeStruct(state.shape, BF),
        ),
        scratch_shapes=[
            pltpu.VMEM(filtered.shape, F32),
            pltpu.VMEM((states, channels), F32),
        ],
        compiler_params=pltpu.CompilerParams(vmem_limit_bytes=24 * 1024 * 1024),
        cost_estimate=pl.CostEstimate(
            flops=2 * tokens * channels * (rank + 4 * states), bytes_accessed=12 * 1024 * 1024, transcendentals=tokens * channels * states
        ),
    )(small, filtered, state, widen, bias.reshape(1, -1), decay_log, skip.reshape(1, -1))


def after(a, b):
    return lax.optimization_barrier((a, b))[0]


def dot(a, b):
    return jnp.dot(a, b, preferred_element_type=F32)


def local(
    hidden,
    shift_state,
    recurrent_row_state,
    input_codes,
    input_scales,
    filter_taps,
    filter_bias,
    narrow_rank_weight,
    coefficient_weight,
    widen_weight,
    step_bias,
    decay_log,
    skip_gain,
    output_codes,
    output_scales,
):
    rows, steps, depth = hidden.shape
    part = rows // HALVES
    span = steps // SPANS
    tok = part * span
    chunks = HALVES * SPANS
    channels = input_codes.shape[2]
    taps = filter_taps.shape[0]
    model = output_codes.shape[1]

    wide = lax.axis_index("wide")
    z = lax.axis_index("narrow")
    core = wide % 2
    x, y = wide // (2 * NY), (wide // 2) % NY
    first_core = core == 0
    sign = 1 - 2 * core
    u = jnp.where(first_core, x, y)
    v = jnp.where(first_core, y, x)

    def by_core(a, b):
        return jnp.where(first_core, a, b), jnp.where(first_core, b, a)

    tokens = hidden.reshape(HALVES, part, steps, depth).transpose(0, 2, 1, 3).reshape(chunks, tok, depth)
    plane = (z + sign * jnp.arange(-3, 5)) % NZ
    want_x = jnp.repeat(plane // 2, 2)
    want_y = (2 * (plane % 2)[:, None] + jnp.arange(2)[None]).reshape(-1)
    want_u = jnp.where(first_core, want_x, want_y)
    want_v = jnp.where(first_core, want_y, want_x)
    gather_index = ((want_v - v) % 4) * 4 + (want_u - u) % 4

    def gather_rows(block, start=None):
        one = jnp.stack([block, shift(block, -1, True), shift(block, 2, True), shift(block, 1, True)])
        up, down = shift(one, -1, False), shift(one, 1, False)
        far = jnp.concatenate([shift(up[:2], -1, False), shift(down[2:], 1, False)])
        two = jnp.concatenate([one, up, far, down])
        if start is not None:
            two = after(two, start)
        mine = pick_blocks([two], gather_index)[:, 0]
        other = swap_cores(mine[:8])
        return mine, other, one, up

    def unpack(mine, other, i):
        return mine[:, i].reshape(8, 2 * tok, depth), other[:, i].reshape(4, 2 * tok, depth)

    token = [None]

    def seq(a):
        if token[0] is not None:
            a = after(a, token[0])
        token[0] = a
        return a

    def sum_over_z(mine, other, p, start=None):
        if start is not None:
            mine = after(mine, start)
        size = mine.shape[1]
        ahead = dot(mine[3:].reshape(5 * size, depth), weight[p]).astype(BF).reshape(5, size, 2 * channels)
        also = dot(other.reshape(4 * size, depth), weight[p]).astype(BF).reshape(4, size, 2 * channels)
        got = ring(ahead[4])
        gots = [got]
        acc = jnp.concatenate([(ahead[3].astype(F32) + got.astype(F32)).astype(BF), also[0]])
        for k in (2, 1):
            got = ring(acc)
            gots.append(got)
            acc = (jnp.concatenate([ahead[k], also[3 - k]]).astype(F32) + got.astype(F32)).astype(BF)
        got = ring(acc)
        swapped = swap_cores(got[:, channels:])
        total = jnp.concatenate([ahead[0], also[3]])[:, :channels].astype(F32) + got[:, :channels].astype(F32)
        total = total + jnp.concatenate([swapped[size:], swapped[:size]]).astype(F32)
        total = total.astype(BF)
        return jnp.concatenate(by_core(total[:size], total[size:])).reshape(4, span, part, channels), gots

    def halves_of(a):
        k = a.shape[1]
        b = a.reshape((2, 2, HALVES, part, k, channels)).transpose(2, 4, 1, 0, 3, 5)
        return [b[h].reshape(k, 4, part, channels) for h in range(HALVES)]

    def rows_of(parts):
        k = parts[0].shape[0]
        b = jnp.stack(parts).reshape(HALVES, k, 2, 2, part, channels)
        return b.transpose(3, 2, 0, 4, 1, 5).reshape(4 * rows, k, channels)

    mine, other, one, up = gather_rows(tokens[:SPANS])

    input_codes = after(input_codes, one)
    w_in = dequantize(input_codes.reshape(depth, 2 * channels), input_scales.reshape(input_scales.shape[0], -1))
    w_in_other = swap_cores(w_in)
    weight = [
        jnp.concatenate([w_in[:, p * channels : (p + 1) * channels], w_in_other[:, p * channels : (p + 1) * channels]], axis=1)
        for p in range(2)
    ]

    lifted, gating, gots, lefts = [], [], [], []
    for h in range(HALVES):
        if h > 0:
            mine, other, one, up = gather_rows(after(tokens[h : h + 1], one))
        lefts.append(unpack(mine, other, 0))
        total, got = sum_over_z(*lefts[h], 0)
        lifted.append(total)
        gots.append(got)
    for h in range(HALVES):
        gating.append(sum_over_z(*lefts[h], 1, gots[h][2])[0])

    shift_state, recurrent_row_state = after((shift_state, recurrent_row_state), gots[0][0])
    w_out = dequantize(after(output_codes, gots[0][1]), output_scales)
    w_down = jnp.concatenate(by_core(w_out, swap_cores(w_out)), axis=0)

    narrow = jnp.concatenate([narrow_rank_weight, coefficient_weight], axis=1)
    width = narrow.shape[1]
    windows = halves_of(shift_state)
    filtered, smalls = [], []
    for h in range(HALVES):
        f, small = causal_filter(lifted[h : h + 1], windows[h], filter_taps, filter_bias, narrow)
        filtered.append(f)
        smalls.append(small)
    small = jnp.stack(smalls)
    mid = small.shape[1] // 2
    keep, give = by_core(small[:, :mid], small[:, mid:])
    total = (keep.astype(F32) + swap_cores(give).astype(F32)).astype(BF)
    for first in (True, False):
        others = [shift(total, d, first) for d in (1, -1, 2)]
        total = sum([o.astype(F32) for o in others], total.astype(F32)).astype(BF)
    smalls = jnp.concatenate(by_core(total, swap_cores(total)), axis=1)
    whole = [jnp.concatenate(lifted[h * SPANS : (h + 1) * SPANS], axis=1) for h in range(HALVES)]
    shift_next = rows_of([jnp.swapaxes(q[:, steps - taps + 1 :], 0, 1) for q in whole])

    state_parts = halves_of(recurrent_row_state)
    scan_parts = []
    e, f = jnp.arange(16) // 4, jnp.arange(16) % 4
    to_u, to_v = (u + e) % 4, (v + f) % 4
    to_x = jnp.where(first_core, to_u, to_v)
    to_y = jnp.where(first_core, to_v, to_u)
    slot = (sign * (z - 2 * to_x - to_y // 2) + 3) % NZ
    target = slot * 2 + to_y % 2

    results = []
    for h in range(HALVES):
        result, state = selective_scan(
            smalls[h], filtered[h], state_parts[h], widen_weight, step_bias, decay_log, skip_gain
        )
        scan_parts.append(state)
        results.append(result)

    near, beyond, known, others = [], [], [], []
    for h in range(HALVES):
        output = (results[h] * jax.nn.silu(gating[h].astype(F32))).astype(BF).reshape(4 * tok, channels)
        output = jnp.concatenate(by_core(output, swap_cores(output)), axis=1)
        mine, theirs = by_core(output[: 2 * tok], output[2 * tok :])
        known.append([mine])
        others.append([])
        beyond.append(mine)
        near.append(theirs)

    for h in range(HALVES):
        beyond[h] = ring(seq(beyond[h]))
        near[h] = ring(seq(near[h]))
    for k in range(3):
        for h in range(HALVES):
            got = seq(beyond[h])
            known[h].append(got)
            beyond[h] = ring(got)
        for h in range(HALVES):
            got = seq(near[h])
            others[h].insert(0, got)
            near[h] = ring(got) if k < 2 else swap_cores(jnp.concatenate(others[h]))

    def project(h):
        last = seq(beyond[h])
        every = jnp.concatenate([near[h]] + known[h] + [last]).reshape(16, tok, 2 * channels)
        picked = pick_blocks([every], target).reshape(16 * tok, 2 * channels)
        return seq(dot(picked, w_down).astype(BF)).reshape(4, 4 * tok, model)

    low = project(0)
    from_low = shift(low[2], 1, True)
    high = project(1)
    from_high = shift(high[2], -1, True)
    up = jnp.concatenate([(low[1].astype(F32) + from_low.astype(F32)).astype(BF), high[1]])
    down = jnp.concatenate([low[3], (high[3].astype(F32) + from_high.astype(F32)).astype(BF)])
    total = jnp.concatenate([low[0], high[0]]).astype(F32)
    total = total + shift(up, 1, True).astype(F32) + shift(down, -1, True).astype(F32)
    total = total.astype(BF).reshape(2, 4, tok, model)
    final = total[:, 0].astype(F32)
    for f, d in ((1, 1), (2, 2), (3, -1)):
        final = final + shift(total[:, f], d, False).astype(F32)

    mixed = final.astype(BF).reshape(HALVES, steps, part, model).transpose(0, 2, 1, 3).reshape(rows, steps, model)
    return (mixed, shift_next, rows_of(scan_parts))


def solution(mesh):
    return jax.shard_map(
        local,
        mesh=mesh,
        in_specs=(
            P("wide", None, "narrow"),
            P("narrow", None, "wide"),
            P("narrow", None, "wide"),
            P("narrow", None, "wide"),
            P("narrow", None, "wide"),
            P(None, "wide"),
            P("wide"),
            P("wide", None),
            P("wide", None),
            P(None, "wide"),
            P("wide"),
            P(None, "wide"),
            P("wide"),
            P("wide", "narrow"),
            P("wide", "narrow"),
        ),
        out_specs=(P("wide", None, "narrow"), P("narrow", None, "wide"), P("narrow", None, "wide")),
        check_vma=False,
    )
```

```python
import math

import jax
import jax.numpy as jnp
from jax import lax
from jax.experimental import pallas as pl
from jax.experimental.pallas import tpu as pltpu
from jax.sharding import PartitionSpec as P

QB = 128
NX, NY, NZ = 4, 4, 8
HALVES = 2
SPANS = 1
BF = jnp.bfloat16
F32 = jnp.float32


def dequantize(codes, scales):
    height, width = codes.shape
    blocks = (
        codes.astype(F32).reshape(height // QB, QB, width // QB, QB)
        * scales[:, None, :, None]
    )
    return blocks.reshape(height, width).astype(BF)


def wide_of(x, y, c):
    return ((x % NX) * NY + (y % NY)) * 2 + c


def swap_cores(a):
    return lax.ppermute(a, "wide", [(w, w ^ 1) for w in range(2 * NX * NY)])


def ring(a):
    pairs = [
        (w * NZ + z, w * NZ + (z + (1 if w % 2 == 0 else -1)) % NZ)
        for w in range(2 * NX * NY)
        for z in range(NZ)
    ]
    return lax.ppermute(a, ("wide", "narrow"), pairs)


def shift(a, step, first):
    pairs = []
    for x in range(NX):
        for y in range(NY):
            for c in range(2):
                if (c == 0) == first:
                    pairs.append((wide_of(x, y, c), wide_of(x + step, y, c)))
                else:
                    pairs.append((wide_of(x, y, c), wide_of(x, y + step, c)))
    return lax.ppermute(a, "wide", pairs)


def pick_blocks(sources, index):
    count = index.shape[0]
    pieces = len(sources)

    def kernel(index_ref, *refs):
        for i in range(count):
            for j in range(pieces):
                refs[-1][i, j] = refs[j][index_ref[i]]

    shape = (count, pieces) + sources[0].shape[1:]
    return pl.pallas_call(
        kernel,
        out_shape=jax.ShapeDtypeStruct(shape, sources[0].dtype),
        in_specs=[pl.BlockSpec(memory_space=pltpu.SMEM)] + [pl.BlockSpec(memory_space=pltpu.VMEM)] * pieces,
        out_specs=pl.BlockSpec(memory_space=pltpu.VMEM),
        compiler_params=pltpu.CompilerParams(vmem_limit_bytes=16 * 1024 * 1024),
        cost_estimate=pl.CostEstimate(flops=0, bytes_accessed=4 * math.prod(shape), transcendentals=0),
    )(index.astype(jnp.int32), *sources)


def causal_filter(pieces, window, taps, bias, narrow):
    blocks, span, part, channels = pieces[0].shape
    steps = span * len(pieces)
    width = narrow.shape[1]
    count = taps.shape[0]

    def kernel(*refs):
        piece_refs = refs[: len(pieces)]
        window_ref, taps_ref, bias_ref, narrow_ref, filtered_ref, small_ref = refs[len(pieces) :]
        for b in range(blocks):
            inputs = [window_ref[k, b].astype(F32) for k in range(count - 1)]
            inputs += [ref[b, t].astype(F32) for ref in piece_refs for t in range(span)]
            for t in range(steps):
                prior = bias_ref[...] + inputs[t] * taps_ref[0:1]
                for k in range(1, count):
                    prior = prior + inputs[t + k] * taps_ref[k : k + 1]
                filtered_ref[b, t] = (prior * jax.nn.sigmoid(prior)).astype(BF)
        left = filtered_ref[...].reshape(blocks * steps * part, channels)
        small_ref[...] = jnp.dot(left, narrow_ref[...], preferred_element_type=F32).astype(BF)

    return pl.pallas_call(
        kernel,
        out_shape=(
            jax.ShapeDtypeStruct((blocks, steps, part, channels), BF),
            jax.ShapeDtypeStruct((blocks * steps * part, width), BF),
        ),
        compiler_params=pltpu.CompilerParams(vmem_limit_bytes=16 * 1024 * 1024),
        cost_estimate=pl.CostEstimate(
            flops=2 * blocks * steps * part * channels * width,
            bytes_accessed=2 * 1024 * 1024,
            transcendentals=blocks * steps * part * channels,
        ),
    )(*pieces, window, taps, bias.reshape(1, -1), narrow)


def selective_scan(small, filtered, state, widen, bias, decay_log, skip):
    blocks, steps, part, channels = filtered.shape
    states = decay_log.shape[0]
    rank = widen.shape[0]
    tile = 256
    tiles = channels // tile

    def kernel(small_ref, filtered_ref, state_ref, widen_ref, bias_ref, decay_ref, skip_ref, result_ref, next_ref, delta_ref, rates_ref):
        value = jnp.dot(small_ref[:, :rank], widen_ref[...], preferred_element_type=F32) + bias_ref[...]
        delta_ref[...] = (jnp.maximum(value, 0.0) + jnp.log1p(jnp.exp(-jnp.abs(value)))).reshape(blocks, steps, part, channels)
        rates_ref[...] = jnp.exp(decay_ref[...]) * (-1.4426950408889634)

        def body(i, carry):
            b = i // tiles
            cols = pl.ds(pl.multiple_of((i % tiles) * tile, tile), tile)
            deltas, inputs, sums = [], [], []
            for t in range(steps):
                x = filtered_ref[b, t, :, cols].astype(F32)
                d = delta_ref[b, t, :, cols]
                deltas.append(d)
                inputs.append(d * x)
                sums.append(skip_ref[:, cols] * x)
            coefs = [
                small_ref[pl.ds(pl.multiple_of((b * steps + t) * part, part), part), rank : rank + 2 * states].astype(F32)
                for t in range(steps)
            ]
            for n in range(states):
                s = state_ref[n, b, :, cols].astype(F32)
                rate = rates_ref[n : n + 1, cols]
                for t in range(steps):
                    s = jnp.exp2(deltas[t] * rate) * s + inputs[t] * coefs[t][:, n : n + 1]
                    sums[t] = sums[t] + s * coefs[t][:, states + n : states + n + 1]
                next_ref[n, b, :, cols] = s.astype(BF)
            for t in range(steps):
                result_ref[b, t, :, cols] = sums[t]
            return carry

        lax.fori_loop(0, blocks * tiles, body, 0)

    tokens = blocks * steps * part
    return pl.pallas_call(
        kernel,
        out_shape=(
            jax.ShapeDtypeStruct(filtered.shape, F32),
            jax.ShapeDtypeStruct(state.shape, BF),
        ),
        scratch_shapes=[
            pltpu.VMEM(filtered.shape, F32),
            pltpu.VMEM((states, channels), F32),
        ],
        compiler_params=pltpu.CompilerParams(vmem_limit_bytes=24 * 1024 * 1024),
        cost_estimate=pl.CostEstimate(
            flops=2 * tokens * channels * (rank + 4 * states), bytes_accessed=12 * 1024 * 1024, transcendentals=tokens * channels * states
        ),
    )(small, filtered, state, widen, bias.reshape(1, -1), decay_log, skip.reshape(1, -1))


def after(a, b):
    return lax.optimization_barrier((a, b))[0]


def dot(a, b):
    return jnp.dot(a, b, preferred_element_type=F32)


def local(
    hidden,
    shift_state,
    recurrent_row_state,
    input_codes,
    input_scales,
    filter_taps,
    filter_bias,
    narrow_rank_weight,
    coefficient_weight,
    widen_weight,
    step_bias,
    decay_log,
    skip_gain,
    output_codes,
    output_scales,
):
    rows, steps, depth = hidden.shape
    part = rows // HALVES
    span = steps // SPANS
    tok = part * span
    chunks = HALVES * SPANS
    channels = input_codes.shape[2]
    taps = filter_taps.shape[0]
    model = output_codes.shape[1]

    wide = lax.axis_index("wide")
    z = lax.axis_index("narrow")
    core = wide % 2
    x, y = wide // (2 * NY), (wide // 2) % NY
    first_core = core == 0
    sign = 1 - 2 * core
    u = jnp.where(first_core, x, y)
    v = jnp.where(first_core, y, x)

    def by_core(a, b):
        return jnp.where(first_core, a, b), jnp.where(first_core, b, a)

    tokens = hidden.reshape(HALVES, part, steps, depth).transpose(0, 2, 1, 3).reshape(chunks, tok, depth)
    plane = (z + sign * jnp.arange(-3, 5)) % NZ
    want_x = jnp.repeat(plane // 2, 2)
    want_y = (2 * (plane % 2)[:, None] + jnp.arange(2)[None]).reshape(-1)
    want_u = jnp.where(first_core, want_x, want_y)
    want_v = jnp.where(first_core, want_y, want_x)
    gather_index = ((want_v - v) % 4) * 4 + (want_u - u) % 4

    def gather_rows(block, start=None):
        one = jnp.stack([block, shift(block, -1, True), shift(block, 2, True), shift(block, 1, True)])
        up, down = shift(one, -1, False), shift(one, 1, False)
        far = jnp.concatenate([shift(up[:2], -1, False), shift(down[2:], 1, False)])
        two = jnp.concatenate([one, up, far, down])
        if start is not None:
            two = after(two, start)
        mine = pick_blocks([two], gather_index)[:, 0]
        other = swap_cores(mine[:8])
        return mine, other, one, up

    def unpack(mine, other, i):
        return mine[:, i].reshape(8, 2 * tok, depth), other[:, i].reshape(4, 2 * tok, depth)

    token = [None]

    def seq(a):
        if token[0] is not None:
            a = after(a, token[0])
        token[0] = a
        return a

    def sum_over_z(mine, other, p, start=None):
        if start is not None:
            mine = after(mine, start)
        size = mine.shape[1]
        ahead = dot(mine[3:].reshape(5 * size, depth), weight[p]).astype(BF).reshape(5, size, 2 * channels)
        also = dot(other.reshape(4 * size, depth), weight[p]).astype(BF).reshape(4, size, 2 * channels)
        got = ring(ahead[4])
        gots = [got]
        acc = jnp.concatenate([(ahead[3].astype(F32) + got.astype(F32)).astype(BF), also[0]])
        for k in (2, 1):
            got = ring(acc)
            gots.append(got)
            acc = (jnp.concatenate([ahead[k], also[3 - k]]).astype(F32) + got.astype(F32)).astype(BF)
        got = ring(acc)
        swapped = swap_cores(got[:, channels:])
        total = jnp.concatenate([ahead[0], also[3]])[:, :channels].astype(F32) + got[:, :channels].astype(F32)
        total = total + jnp.concatenate([swapped[size:], swapped[:size]]).astype(F32)
        total = total.astype(BF)
        return jnp.concatenate(by_core(total[:size], total[size:])).reshape(4, span, part, channels), gots

    def halves_of(a):
        k = a.shape[1]
        b = a.reshape((2, 2, HALVES, part, k, channels)).transpose(2, 4, 1, 0, 3, 5)
        return [b[h].reshape(k, 4, part, channels) for h in range(HALVES)]

    def rows_of(parts):
        k = parts[0].shape[0]
        b = jnp.stack(parts).reshape(HALVES, k, 2, 2, part, channels)
        return b.transpose(3, 2, 0, 4, 1, 5).reshape(4 * rows, k, channels)

    mine, other, one, up = gather_rows(tokens[:SPANS])

    input_codes = after(input_codes, one)
    w_in = dequantize(input_codes.reshape(depth, 2 * channels), input_scales.reshape(input_scales.shape[0], -1))
    w_in_other = swap_cores(w_in)
    weight = [
        jnp.concatenate([w_in[:, p * channels : (p + 1) * channels], w_in_other[:, p * channels : (p + 1) * channels]], axis=1)
        for p in range(2)
    ]

    lifted, gating, gots, lefts = [], [], [], []
    for h in range(HALVES):
        if h > 0:
            mine, other, one, up = gather_rows(after(tokens[h : h + 1], one))
        lefts.append(unpack(mine, other, 0))
        total, got = sum_over_z(*lefts[h], 0)
        lifted.append(total)
        gots.append(got)
    for h in range(HALVES):
        gating.append(sum_over_z(*lefts[h], 1, gots[h][2])[0])

    shift_state, recurrent_row_state = after((shift_state, recurrent_row_state), gots[0][0])
    w_out = dequantize(after(output_codes, gots[0][1]), output_scales)
    w_down = jnp.concatenate(by_core(w_out, swap_cores(w_out)), axis=0)

    narrow = jnp.concatenate([narrow_rank_weight, coefficient_weight], axis=1)
    width = narrow.shape[1]
    windows = halves_of(shift_state)
    filtered, smalls = [], []
    for h in range(HALVES):
        f, small = causal_filter(lifted[h : h + 1], windows[h], filter_taps, filter_bias, narrow)
        filtered.append(f)
        smalls.append(small)
    small = jnp.stack(smalls)
    mid = small.shape[1] // 2
    keep, give = by_core(small[:, :mid], small[:, mid:])
    total = (keep.astype(F32) + swap_cores(give).astype(F32)).astype(BF)
    for first in (True, False):
        others = [shift(total, d, first) for d in (1, -1, 2)]
        total = sum([o.astype(F32) for o in others], total.astype(F32)).astype(BF)
    smalls = jnp.concatenate(by_core(total, swap_cores(total)), axis=1)
    whole = [jnp.concatenate(lifted[h * SPANS : (h + 1) * SPANS], axis=1) for h in range(HALVES)]
    shift_next = rows_of([jnp.swapaxes(q[:, steps - taps + 1 :], 0, 1) for q in whole])

    state_parts = halves_of(recurrent_row_state)
    scan_parts = []
    e, f = jnp.arange(16) // 4, jnp.arange(16) % 4
    to_u, to_v = (u + e) % 4, (v + f) % 4
    to_x = jnp.where(first_core, to_u, to_v)
    to_y = jnp.where(first_core, to_v, to_u)
    slot = (sign * (z - 2 * to_x - to_y // 2) + 3) % NZ
    target = slot * 2 + to_y % 2

    results = []
    for h in range(HALVES):
        result, state = selective_scan(
            smalls[h], filtered[h], state_parts[h], widen_weight, step_bias, decay_log, skip_gain
        )
        scan_parts.append(state)
        results.append(result)

    near, beyond, known, others = [], [], [], []
    for h in range(HALVES):
        output = (results[h] * jax.nn.silu(gating[h].astype(F32))).astype(BF).reshape(4 * tok, channels)
        output = jnp.concatenate(by_core(output, swap_cores(output)), axis=1)
        mine, theirs = by_core(output[: 2 * tok], output[2 * tok :])
        known.append([mine])
        others.append([])
        beyond.append(mine)
        near.append(theirs)

    for h in range(HALVES):
        beyond[h] = ring(seq(beyond[h]))
        near[h] = ring(seq(near[h]))
    def pass_on(h):
        got = seq(beyond[h])
        known[h].append(got)
        beyond[h] = ring(got)

    def pass_near(h, k):
        got = seq(near[h])
        others[h].insert(0, got)
        near[h] = ring(got) if k < 2 else swap_cores(jnp.concatenate(others[h]))

    for k in range(2):
        for h in range(HALVES):
            pass_on(h)
        for h in range(HALVES):
            pass_near(h, k)
    pass_on(0)
    pass_on(1)
    pass_near(0, 2)
    lasts = [seq(beyond[0])]
    pass_near(1, 2)

    def project(h):
        if h > 0:
            lasts.append(seq(beyond[h]))
        last = lasts[h]
        every = jnp.concatenate([near[h]] + known[h] + [last]).reshape(16, tok, 2 * channels)
        picked = pick_blocks([every], target).reshape(16 * tok, 2 * channels)
        return seq(dot(picked, w_down).astype(BF)).reshape(4, 4 * tok, model)

    low = project(0)
    from_low = shift(low[2], 1, True)
    low_down = shift(low[3], -1, True)
    high = project(1)
    from_high = shift(high[2], -1, True)
    high_up = shift(high[1], 1, True)
    low_up = shift((low[1].astype(F32) + from_low.astype(F32)).astype(BF), 1, True)
    high_down = shift((high[3].astype(F32) + from_high.astype(F32)).astype(BF), -1, True)
    total = jnp.concatenate([low[0], high[0]]).astype(F32)
    total = total + jnp.concatenate([low_up, high_up]).astype(F32) + jnp.concatenate([low_down, high_down]).astype(F32)
    total = total.astype(BF).reshape(2, 4, tok, model)
    final = total[:, 0].astype(F32)
    for f, d in ((1, 1), (2, 2), (3, -1)):
        final = final + shift(total[:, f], d, False).astype(F32)

    mixed = final.astype(BF).reshape(HALVES, steps, part, model).transpose(0, 2, 1, 3).reshape(rows, steps, model)
    return (mixed, shift_next, rows_of(scan_parts))


def solution(mesh):
    return jax.shard_map(
        local,
        mesh=mesh,
        in_specs=(
            P("wide", None, "narrow"),
            P("narrow", None, "wide"),
            P("narrow", None, "wide"),
            P("narrow", None, "wide"),
            P("narrow", None, "wide"),
            P(None, "wide"),
            P("wide"),
            P("wide", None),
            P("wide", None),
            P(None, "wide"),
            P("wide"),
            P(None, "wide"),
            P("wide"),
            P("wide", "narrow"),
            P("wide", "narrow"),
        ),
        out_specs=(P("wide", None, "narrow"), P("narrow", None, "wide"), P("narrow", None, "wide")),
        check_vma=False,
    )
```

```python
import math

import jax
import jax.numpy as jnp
from jax import lax
from jax.experimental import pallas as pl
from jax.experimental.pallas import tpu as pltpu
from jax.sharding import PartitionSpec as P

QB = 128
NX, NY, NZ = 4, 4, 8
HALVES = 2
SPANS = 1
BF = jnp.bfloat16
F32 = jnp.float32


def dequantize(codes, scales):
    height, width = codes.shape
    blocks = (
        codes.astype(F32).reshape(height // QB, QB, width // QB, QB)
        * scales[:, None, :, None]
    )
    return blocks.reshape(height, width).astype(BF)


def wide_of(x, y, c):
    return ((x % NX) * NY + (y % NY)) * 2 + c


def swap_cores(a):
    return lax.ppermute(a, "wide", [(w, w ^ 1) for w in range(2 * NX * NY)])


def ring(a):
    pairs = [
        (w * NZ + z, w * NZ + (z + (1 if w % 2 == 0 else -1)) % NZ)
        for w in range(2 * NX * NY)
        for z in range(NZ)
    ]
    return lax.ppermute(a, ("wide", "narrow"), pairs)


def shift(a, step, first):
    pairs = []
    for x in range(NX):
        for y in range(NY):
            for c in range(2):
                if (c == 0) == first:
                    pairs.append((wide_of(x, y, c), wide_of(x + step, y, c)))
                else:
                    pairs.append((wide_of(x, y, c), wide_of(x, y + step, c)))
    return lax.ppermute(a, "wide", pairs)


def pick_blocks(sources, index):
    count = index.shape[0]
    pieces = len(sources)

    def kernel(index_ref, *refs):
        for i in range(count):
            for j in range(pieces):
                refs[-1][i, j] = refs[j][index_ref[i]]

    shape = (count, pieces) + sources[0].shape[1:]
    return pl.pallas_call(
        kernel,
        out_shape=jax.ShapeDtypeStruct(shape, sources[0].dtype),
        in_specs=[pl.BlockSpec(memory_space=pltpu.SMEM)] + [pl.BlockSpec(memory_space=pltpu.VMEM)] * pieces,
        out_specs=pl.BlockSpec(memory_space=pltpu.VMEM),
        compiler_params=pltpu.CompilerParams(vmem_limit_bytes=16 * 1024 * 1024),
        cost_estimate=pl.CostEstimate(flops=0, bytes_accessed=4 * math.prod(shape), transcendentals=0),
    )(index.astype(jnp.int32), *sources)


def causal_filter(pieces, window, taps, bias, narrow):
    blocks, span, part, channels = pieces[0].shape
    steps = span * len(pieces)
    width = narrow.shape[1]
    count = taps.shape[0]

    def kernel(*refs):
        piece_refs = refs[: len(pieces)]
        window_ref, taps_ref, bias_ref, narrow_ref, filtered_ref, small_ref = refs[len(pieces) :]
        for b in range(blocks):
            inputs = [window_ref[k, b].astype(F32) for k in range(count - 1)]
            inputs += [ref[b, t].astype(F32) for ref in piece_refs for t in range(span)]
            for t in range(steps):
                prior = bias_ref[...] + inputs[t] * taps_ref[0:1]
                for k in range(1, count):
                    prior = prior + inputs[t + k] * taps_ref[k : k + 1]
                filtered_ref[b, t] = (prior * jax.nn.sigmoid(prior)).astype(BF)
        left = filtered_ref[...].reshape(blocks * steps * part, channels)
        small_ref[...] = jnp.dot(left, narrow_ref[...], preferred_element_type=F32).astype(BF)

    return pl.pallas_call(
        kernel,
        out_shape=(
            jax.ShapeDtypeStruct((blocks, steps, part, channels), BF),
            jax.ShapeDtypeStruct((blocks * steps * part, width), BF),
        ),
        compiler_params=pltpu.CompilerParams(vmem_limit_bytes=16 * 1024 * 1024),
        cost_estimate=pl.CostEstimate(
            flops=2 * blocks * steps * part * channels * width,
            bytes_accessed=2 * 1024 * 1024,
            transcendentals=blocks * steps * part * channels,
        ),
    )(*pieces, window, taps, bias.reshape(1, -1), narrow)


def selective_scan(small, filtered, state, widen, bias, decay_log, skip):
    blocks, steps, part, channels = filtered.shape
    states = decay_log.shape[0]
    rank = widen.shape[0]
    tile = 256
    tiles = channels // tile

    def kernel(small_ref, filtered_ref, state_ref, widen_ref, bias_ref, decay_ref, skip_ref, result_ref, next_ref, delta_ref, rates_ref):
        value = jnp.dot(small_ref[:, :rank], widen_ref[...], preferred_element_type=F32) + bias_ref[...]
        delta_ref[...] = (jnp.maximum(value, 0.0) + jnp.log1p(jnp.exp(-jnp.abs(value)))).reshape(blocks, steps, part, channels)
        rates_ref[...] = jnp.exp(decay_ref[...]) * (-1.4426950408889634)

        def body(i, carry):
            b = i // tiles
            cols = pl.ds(pl.multiple_of((i % tiles) * tile, tile), tile)
            deltas, inputs, sums = [], [], []
            for t in range(steps):
                x = filtered_ref[b, t, :, cols].astype(F32)
                d = delta_ref[b, t, :, cols]
                deltas.append(d)
                inputs.append(d * x)
                sums.append(skip_ref[:, cols] * x)
            coefs = [
                small_ref[pl.ds(pl.multiple_of((b * steps + t) * part, part), part), rank : rank + 2 * states].astype(F32)
                for t in range(steps)
            ]
            for n in range(states):
                s = state_ref[n, b, :, cols].astype(F32)
                rate = rates_ref[n : n + 1, cols]
                for t in range(steps):
                    s = jnp.exp2(deltas[t] * rate) * s + inputs[t] * coefs[t][:, n : n + 1]
                    sums[t] = sums[t] + s * coefs[t][:, states + n : states + n + 1]
                next_ref[n, b, :, cols] = s.astype(BF)
            for t in range(steps):
                result_ref[b, t, :, cols] = sums[t]
            return carry

        lax.fori_loop(0, blocks * tiles, body, 0)

    tokens = blocks * steps * part
    return pl.pallas_call(
        kernel,
        out_shape=(
            jax.ShapeDtypeStruct(filtered.shape, F32),
            jax.ShapeDtypeStruct(state.shape, BF),
        ),
        scratch_shapes=[
            pltpu.VMEM(filtered.shape, F32),
            pltpu.VMEM((states, channels), F32),
        ],
        compiler_params=pltpu.CompilerParams(vmem_limit_bytes=24 * 1024 * 1024),
        cost_estimate=pl.CostEstimate(
            flops=2 * tokens * channels * (rank + 4 * states), bytes_accessed=12 * 1024 * 1024, transcendentals=tokens * channels * states
        ),
    )(small, filtered, state, widen, bias.reshape(1, -1), decay_log, skip.reshape(1, -1))


def after(a, b):
    return lax.optimization_barrier((a, b))[0]


def dot(a, b):
    return jnp.dot(a, b, preferred_element_type=F32)


def local(
    hidden,
    shift_state,
    recurrent_row_state,
    input_codes,
    input_scales,
    filter_taps,
    filter_bias,
    narrow_rank_weight,
    coefficient_weight,
    widen_weight,
    step_bias,
    decay_log,
    skip_gain,
    output_codes,
    output_scales,
):
    rows, steps, depth = hidden.shape
    part = rows // HALVES
    span = steps // SPANS
    tok = part * span
    chunks = HALVES * SPANS
    channels = input_codes.shape[2]
    taps = filter_taps.shape[0]
    model = output_codes.shape[1]

    wide = lax.axis_index("wide")
    z = lax.axis_index("narrow")
    core = wide % 2
    x, y = wide // (2 * NY), (wide // 2) % NY
    first_core = core == 0
    sign = 1 - 2 * core
    u = jnp.where(first_core, x, y)
    v = jnp.where(first_core, y, x)

    def by_core(a, b):
        return jnp.where(first_core, a, b), jnp.where(first_core, b, a)

    tokens = hidden.reshape(HALVES, part, steps, depth).transpose(0, 2, 1, 3).reshape(chunks, tok, depth)
    plane = (z + sign * jnp.arange(-3, 5)) % NZ
    want_x = jnp.repeat(plane // 2, 2)
    want_y = (2 * (plane % 2)[:, None] + jnp.arange(2)[None]).reshape(-1)
    want_u = jnp.where(first_core, want_x, want_y)
    want_v = jnp.where(first_core, want_y, want_x)
    gather_index = ((want_v - v) % 4) * 4 + (want_u - u) % 4

    def gather_rows(block, start=None):
        one = jnp.stack([block, shift(block, -1, True), shift(block, 2, True), shift(block, 1, True)])
        up, down = shift(one, -1, False), shift(one, 1, False)
        far = jnp.concatenate([shift(up[:2], -1, False), shift(down[2:], 1, False)])
        two = jnp.concatenate([one, up, far, down])
        if start is not None:
            two = after(two, start)
        mine = pick_blocks([two], gather_index)[:, 0]
        other = swap_cores(mine[:8])
        return mine, other, one, up

    def unpack(mine, other, i):
        return mine[:, i].reshape(8, 2 * tok, depth), other[:, i].reshape(4, 2 * tok, depth)

    token = [None]

    def seq(a):
        if token[0] is not None:
            a = after(a, token[0])
        token[0] = a
        return a

    def sum_over_z(mine, other, p, start=None):
        if start is not None:
            mine = after(mine, start)
        size = mine.shape[1]
        ahead = dot(mine[3:].reshape(5 * size, depth), weight[p]).astype(BF).reshape(5, size, 2 * channels)
        also = dot(other.reshape(4 * size, depth), weight[p]).astype(BF).reshape(4, size, 2 * channels)
        got = ring(ahead[4])
        gots = [got]
        acc = jnp.concatenate([(ahead[3].astype(F32) + got.astype(F32)).astype(BF), also[0]])
        for k in (2, 1):
            got = ring(acc)
            gots.append(got)
            acc = (jnp.concatenate([ahead[k], also[3 - k]]).astype(F32) + got.astype(F32)).astype(BF)
        got = ring(acc)
        swapped = swap_cores(got[:, channels:])
        total = jnp.concatenate([ahead[0], also[3]])[:, :channels].astype(F32) + got[:, :channels].astype(F32)
        total = total + jnp.concatenate([swapped[size:], swapped[:size]]).astype(F32)
        total = total.astype(BF)
        return jnp.concatenate(by_core(total[:size], total[size:])).reshape(4, span, part, channels), gots

    def halves_of(a):
        k = a.shape[1]
        b = a.reshape((2, 2, HALVES, part, k, channels)).transpose(2, 4, 1, 0, 3, 5)
        return [b[h].reshape(k, 4, part, channels) for h in range(HALVES)]

    def rows_of(parts):
        k = parts[0].shape[0]
        b = jnp.stack(parts).reshape(HALVES, k, 2, 2, part, channels)
        return b.transpose(3, 2, 0, 4, 1, 5).reshape(4 * rows, k, channels)

    mine, other, one, up = gather_rows(tokens[:SPANS])

    input_codes = after(input_codes, one)
    w_in = dequantize(input_codes.reshape(depth, 2 * channels), input_scales.reshape(input_scales.shape[0], -1))
    w_in_other = swap_cores(w_in)
    weight = [
        jnp.concatenate([w_in[:, p * channels : (p + 1) * channels], w_in_other[:, p * channels : (p + 1) * channels]], axis=1)
        for p in range(2)
    ]

    lifted, gating, gots, lefts = [], [], [], []
    for h in range(HALVES):
        if h > 0:
            mine, other, one, up = gather_rows(after(tokens[h : h + 1], up))
        lefts.append(unpack(mine, other, 0))
        total, got = sum_over_z(*lefts[h], 0)
        lifted.append(total)
        gots.append(got)
    for h in range(HALVES):
        gating.append(sum_over_z(*lefts[h], 1, gots[h][2])[0])

    shift_state, recurrent_row_state = after((shift_state, recurrent_row_state), gots[0][0])
    w_out = dequantize(after(output_codes, gots[0][1]), output_scales)
    w_down = jnp.concatenate(by_core(w_out, swap_cores(w_out)), axis=0)

    narrow = jnp.concatenate([narrow_rank_weight, coefficient_weight], axis=1)
    width = narrow.shape[1]
    windows = halves_of(shift_state)
    filtered, smalls = [], []
    for h in range(HALVES):
        f, small = causal_filter(lifted[h : h + 1], windows[h], filter_taps, filter_bias, narrow)
        filtered.append(f)
        smalls.append(small)
    small = jnp.stack(smalls)
    mid = small.shape[1] // 2
    keep, give = by_core(small[:, :mid], small[:, mid:])
    total = (keep.astype(F32) + swap_cores(give).astype(F32)).astype(BF)
    for first in (True, False):
        others = [shift(total, d, first) for d in (1, -1, 2)]
        total = sum([o.astype(F32) for o in others], total.astype(F32)).astype(BF)
    smalls = jnp.concatenate(by_core(total, swap_cores(total)), axis=1)
    whole = [jnp.concatenate(lifted[h * SPANS : (h + 1) * SPANS], axis=1) for h in range(HALVES)]
    shift_next = rows_of([jnp.swapaxes(q[:, steps - taps + 1 :], 0, 1) for q in whole])

    state_parts = halves_of(recurrent_row_state)
    scan_parts = []
    e, f = jnp.arange(16) // 4, jnp.arange(16) % 4
    to_u, to_v = (u + e) % 4, (v + f) % 4
    to_x = jnp.where(first_core, to_u, to_v)
    to_y = jnp.where(first_core, to_v, to_u)
    slot = (sign * (z - 2 * to_x - to_y // 2) + 3) % NZ
    target = slot * 2 + to_y % 2

    results = []
    for h in range(HALVES):
        result, state = selective_scan(
            smalls[h], filtered[h], state_parts[h], widen_weight, step_bias, decay_log, skip_gain
        )
        scan_parts.append(state)
        results.append(result)

    near, beyond, known, others = [], [], [], []
    for h in range(HALVES):
        output = (results[h] * jax.nn.silu(gating[h].astype(F32))).astype(BF).reshape(4 * tok, channels)
        output = jnp.concatenate(by_core(output, swap_cores(output)), axis=1)
        mine, theirs = by_core(output[: 2 * tok], output[2 * tok :])
        known.append([mine])
        others.append([])
        beyond.append(mine)
        near.append(theirs)

    for h in range(HALVES):
        beyond[h] = ring(seq(beyond[h]))
        near[h] = ring(seq(near[h]))
    def pass_on(h):
        got = seq(beyond[h])
        known[h].append(got)
        beyond[h] = ring(got)

    def pass_near(h, k):
        got = seq(near[h])
        others[h].insert(0, got)
        near[h] = ring(got) if k < 2 else swap_cores(jnp.concatenate(others[h]))

    for k in range(2):
        for h in range(HALVES):
            pass_on(h)
        for h in range(HALVES):
            pass_near(h, k)
    pass_on(0)
    pass_on(1)
    pass_near(0, 2)
    lasts = [seq(beyond[0])]
    pass_near(1, 2)

    def project(h):
        if h > 0:
            lasts.append(seq(beyond[h]))
        last = lasts[h]
        every = jnp.concatenate([near[h]] + known[h] + [last]).reshape(16, tok, 2 * channels)
        picked = pick_blocks([every], target).reshape(16 * tok, 2 * channels)
        return seq(dot(picked, w_down).astype(BF)).reshape(4, 4 * tok, model)

    low = project(0)
    from_low = shift(low[2], 1, True)
    low_down = shift(low[3], -1, True)
    high = project(1)
    from_high = shift(high[2], -1, True)
    high_up = shift(high[1], 1, True)
    low_up = shift((low[1].astype(F32) + from_low.astype(F32)).astype(BF), 1, True)
    high_down = shift((high[3].astype(F32) + from_high.astype(F32)).astype(BF), -1, True)
    total = jnp.concatenate([low[0], high[0]]).astype(F32)
    total = total + jnp.concatenate([low_up, high_up]).astype(F32) + jnp.concatenate([low_down, high_down]).astype(F32)
    total = total.astype(BF).reshape(2, 4, tok, model)
    final = total[:, 0].astype(F32)
    for f, d in ((1, 1), (2, 2), (3, -1)):
        final = final + shift(total[:, f], d, False).astype(F32)

    mixed = final.astype(BF).reshape(HALVES, steps, part, model).transpose(0, 2, 1, 3).reshape(rows, steps, model)
    return (mixed, shift_next, rows_of(scan_parts))


def solution(mesh):
    return jax.shard_map(
        local,
        mesh=mesh,
        in_specs=(
            P("wide", None, "narrow"),
            P("narrow", None, "wide"),
            P("narrow", None, "wide"),
            P("narrow", None, "wide"),
            P("narrow", None, "wide"),
            P(None, "wide"),
            P("wide"),
            P("wide", None),
            P("wide", None),
            P(None, "wide"),
            P("wide"),
            P(None, "wide"),
            P("wide"),
            P("wide", "narrow"),
            P("wide", "narrow"),
        ),
        out_specs=(P("wide", None, "narrow"), P("narrow", None, "wide"), P("narrow", None, "wide")),
        check_vma=False,
    )
```
